32 devices in a mesh: col: 16 (over z, y, x), row: 2 (over core).
Axes of the slice: x: 2, y: 2, z: 4, core: 2. Of those that a mesh axis runs over, the one named last changes fastest.
Arguments:
- k_blocks: bfloat16 [2, 16, 4, 256, 256], P('row', 'col'), may hold values from -0.1875 to 0.1875
- slot_row: int32 [2, 16, 4], P('row', 'col'), may hold values from 0 to 3
- slot_col: int32 [2, 16, 4], P('row', 'col'), may hold values from 0 to 3
- live_count: int32 [2, 16], P('row', 'col'), may hold values from 1 to 4, as said below
- cost: float32 [16384], P('col'), may hold values from -6 to 6
- upper: float32 [16384], P('col'), may hold values from 0.5 to 2
- tau: float32 [16384], P('col'), may hold values from 0.2 to 0.8
- sigma: float32 [2, 1024], P('row', 'col'), may hold values from 0.2 to 0.8
- demand: float32 [2, 1024, 128], P('row', 'col'), may hold values from -6 to 6
- primal_start: float32 [16384, 128], P('col'), may hold values from 0 to 1
- dual_start: float32 [2, 1024, 128], P('row', 'col'), may hold values from 0 to 1
Outputs:
- primal: float32 [16384, 128], P('col')
- dual: float32 [2, 1024, 128], P('row', 'col')
The draws below stay inside these ranges and needn't reach their ends.
Inputs may be any that keep to these rules, and one draw needn't show every extreme that they name: `live_count`: only slots below a device's count belong to K; the blocks in later slots are ignored. Some device has all 4 slots in use.
All inputs are finite; a program needn't handle non-finite values.
Results may differ from the reference program's by a relative error of at most 0.0023.
Values may be sent and summed in bfloat16 or wider, within the bound.
A program may use at most 64 MiB of HBM per device.

```python
import math
import jax
import jax.numpy as jnp
from jax import lax

S = 128
BS = 256
CBD = 4
NBD = 4
ITERS = 2
RBG = 4
NVAR = 16384
NGROUPROWS = 1024
N_COL = 16
N_ROW = 2


def draw_live_count(key, part):
    total = N_ROW * N_COL
    shifts = jax.random.randint(key, (total,), 0, 3)
    counts = jnp.maximum(NBD // 2 ** shifts, 1)
    order = jax.random.permutation(jax.random.fold_in(key, 7), total)
    counts = counts.at[order[0]].set(NBD).at[order[1]].set(max(1, NBD // 4))
    return counts.reshape(N_ROW, N_COL).astype(jnp.int32)


def place_ends(drawn, stream_key, smallest, top_value):
    extent = drawn.shape
    place = [jax.random.randint(jax.random.fold_in(stream_key, axis), (), 0, extent[axis]) for axis in range(len(extent))]
    drawn = drawn.at[tuple(place)].set(smallest)
    longest = extent.index(max(extent))
    place[longest] = (place[longest] + 1) % extent[longest]
    return drawn.at[tuple(place)].set(top_value)


def level_of(own_key, shape, pieces, least, top_value):
    def one(axis_at, parts):
        heights = jax.random.uniform(jax.random.fold_in(jax.random.fold_in(own_key, 6), axis_at), (parts,), jnp.float32, least / len(pieces), top_value / len(pieces))
        return jnp.repeat(jnp.exp(heights), shape[axis_at] // parts).reshape((-1,) + (1,) * (len(shape) - axis_at - 1))

    factor_of = one(*pieces[0])
    for cut in pieces[1:]:
        factor_of = factor_of * one(*cut)
    return factor_of


def noise(own_key, shape, scale, reach, pieces=(), kind=jnp.bfloat16):
    drawn = jax.random.normal(own_key, shape, jnp.float32) * scale
    if len(pieces) > 0:
        drawn = level_of(own_key, shape, pieces, -0.22, 0.18) * drawn
    return jnp.clip(drawn, min=-reach, max=reach).astype(kind)


def setup_inputs(seed: int = 0) -> dict:
    keys = jax.random.split(jax.random.key(seed), 12)
    return {
        "k_blocks": noise(keys[0], (N_ROW, N_COL, NBD, BS, BS), (BS * NBD) ** -0.5, 0.1875, ((0, 2), (1, 16))),
        "slot_row": place_ends(jax.random.randint(keys[1], (N_ROW, N_COL, NBD), 0, RBG), jax.random.fold_in(keys[1], 1), 0, RBG - 1).astype(jnp.int32),
        "slot_col": place_ends(jax.random.randint(keys[2], (N_ROW, N_COL, NBD), 0, CBD), jax.random.fold_in(keys[2], 1), 0, CBD - 1).astype(jnp.int32),
        "live_count": draw_live_count(jax.random.fold_in(keys[11], 71), 0),
        "cost": noise(keys[4], (NVAR,), 1.0, 6.0, ((0, 16),), jnp.float32),
        "upper": jnp.clip(jnp.exp(math.log(2.0) - 1.3862944 * jax.random.uniform(keys[5], (NVAR,), jnp.float32) ** level_of(keys[5], (NVAR,), ((0, 16),), -0.2, 0.2)), 0.5, 2.0),
        "tau": jnp.clip(jnp.exp(math.log(0.8) - 1.3862944 * jax.random.uniform(keys[6], (NVAR,), jnp.float32) ** level_of(keys[6], (NVAR,), ((0, 16),), -0.2, 0.2)), 0.2, 0.8),
        "sigma": jnp.clip(jnp.exp(math.log(0.8) - 1.3862944 * jax.random.uniform(keys[7], (N_ROW, NGROUPROWS), jnp.float32) ** level_of(keys[7], (N_ROW, NGROUPROWS), ((0, 2), (1, 16)), -0.2, 0.2)), 0.2, 0.8),
        "demand": noise(keys[8], (N_ROW, NGROUPROWS, S), 1.0, 6.0, ((0, 2), (1, 16)), jnp.float32),
        "primal_start": jnp.clip(1.0 * jax.random.uniform(keys[9], (NVAR, S), jnp.float32) ** level_of(keys[9], (NVAR, S), ((0, 16),), -0.2, 0.2), 0.0, 1.0),
        "dual_start": jnp.clip(1.0 * jax.random.uniform(keys[10], (N_ROW, NGROUPROWS, S), jnp.float32) ** level_of(keys[10], (N_ROW, NGROUPROWS, S), ((0, 2), (1, 16)), -0.2, 0.2), 0.0, 1.0),
    }


def reference(k_blocks, slot_row, slot_col, live_count, cost, upper, tau, sigma, demand, primal_start, dual_start):
    live = jnp.arange(NBD)[None, None, :] < live_count[:, :, None]
    row_hot = ((slot_row[..., None] == jnp.arange(RBG)[None, None, None, :]) & live[..., None]).astype(jnp.float32)
    col_hot = ((slot_col[..., None] == jnp.arange(CBD)[None, None, None, :]) & live[..., None]).astype(jnp.float32)
    row_ids = jnp.arange(N_ROW).astype(jnp.int32)
    col_ids = jnp.arange(N_COL).astype(jnp.int32)

    def transpose_product(dual_low):
        grouped = dual_low.reshape(N_ROW, RBG, BS, S)

        def one_column(index):
            blocks = k_blocks[:, index].astype(jnp.float32)
            picks = grouped[row_ids[:, None], slot_row[:, index]].astype(jnp.float32)
            terms = jnp.einsum("rkij,rkis->rkjs", blocks, picks)
            return jnp.einsum("rkc,rkjs->cjs", col_hot[:, index], terms, precision=lax.Precision.HIGHEST)

        return lax.map(one_column, col_ids).reshape(NVAR, S)

    def forward_product(extrapolated):
        grouped = extrapolated.reshape(N_COL, CBD, BS, S)

        def one_group(index):
            blocks = k_blocks[index].astype(jnp.float32)
            picks = grouped[col_ids[:, None], slot_col[index]].astype(jnp.float32)
            terms = jnp.einsum("ckij,ckjs->ckis", blocks, picks)
            rows = jnp.einsum("ckg,ckis->gis", row_hot[index], terms, precision=lax.Precision.HIGHEST)
            return rows.reshape(NGROUPROWS, S)

        return lax.map(one_group, row_ids)

    primal = primal_start
    dual = dual_start
    for step in range(ITERS):
        dual_low = dual.astype(jnp.bfloat16)
        back = transpose_product(dual_low)
        new_primal = jnp.minimum(jnp.maximum(primal - tau[:, None] * (cost[:, None] - back), 0.0), upper[:, None])
        extrapolated = (2.0 * new_primal - primal).astype(jnp.bfloat16)
        forward = forward_product(extrapolated)
        dual = jnp.maximum(dual + sigma[:, :, None] * (demand - forward), 0.0)
        primal = new_primal
    return primal, dual
```

```python
import functools

import jax
import jax.numpy as jnp
from jax import lax
from jax.experimental import pallas as pl
from jax.experimental.pallas import tpu as pltpu
from jax.sharding import PartitionSpec as P

ITERS = 2
MESH = pl.DeviceIdType.MESH
F32 = jnp.float32
BF16 = jnp.bfloat16


def spread(vector, lanes):
    n = vector.shape[1]
    at_row = lax.broadcasted_iota(jnp.int32, (n, n), 0)
    at_col = lax.broadcasted_iota(jnp.int32, (n, n), 1)
    picked = jnp.where(at_row == at_col, jnp.broadcast_to(vector, (n, n)), 0.0)
    return jnp.broadcast_to(jnp.sum(picked, axis=1, keepdims=True), (n, lanes))


def kernel(
    sizes,
    slot_row,
    slot_col,
    live_count,
    k_hbm,
    cost_ref,
    upper_ref,
    tau_ref,
    sigma_ref,
    demand_hbm,
    primal_hbm,
    dual_hbm,
    primal_out,
    dual_out,
    blocks,
    blocks_t,
    primal,
    dual,
    demand,
    cost,
    upper,
    tau,
    sigma,
    terms,
    extrapolated,
    everyones,
    pairs,
    outgoings,
    plane_ins,
    column_outs,
    column_ins,
    local_sem,
    gather_send,
    gather_recv,
    pair_send,
    pair_recv,
    plane_send,
    plane_recv,
    column_send,
    column_recv,
):
    zs, ps, rs = sizes
    slots, width, _ = blocks.shape
    own = width // ps
    col_blocks = extrapolated.shape[0]
    scenarios = dual.shape[1]
    col = lax.axis_index("col")
    row = lax.axis_index("row")
    z, p = col // ps, lax.rem(col, ps)

    def z_peer(d):
        return {"col": lax.rem(z + d, zs) * ps + p}

    def p_peer(e):
        return {"col": z * ps + lax.rem(p + e, ps)}

    def r_peer(f):
        return {"row": lax.rem(row + f, rs)}

    def back_z(d):
        return lax.rem(z - d + zs, zs)

    mine = pl.ds(pl.multiple_of(p * own, own), own)

    loads = [
        pltpu.make_async_copy(src, dst, local_sem.at[i])
        for i, (src, dst) in enumerate(
            (
                (dual_hbm.at[0], dual),
                (k_hbm.at[0, 0], blocks),
                (primal_hbm, primal),
                (demand_hbm.at[0], demand),
            )
        )
    ]
    for load in loads:
        load.start()

    barrier = pltpu.get_barrier_semaphore()
    peers = (
        [z_peer(d) for d in range(1, zs)]
        + [p_peer(e) for e in range(1, ps)]
        + [r_peer(f) for f in range(1, rs)]
    )
    for peer in peers:
        pl.semaphore_signal(barrier, inc=1, device_id=peer, device_id_type=MESH)

    live = live_count[0, 0]
    alive = [k < live for k in range(slots)]
    rows_of = [slot_row[0, 0, k] for k in range(slots)]
    cols_of = [slot_col[0, 0, k] for k in range(slots)]

    loads[0].wait()
    everyones[0][z, mine, :] = dual[...].astype(BF16)

    chunk = cost_ref.shape[1]
    for i in range(cost_ref.shape[0]):
        at = pl.ds(i * chunk, chunk)
        cost[at, :] = spread(cost_ref[i : i + 1, :], scenarios)
        upper[at, :] = spread(upper_ref[i : i + 1, :], scenarios)
        tau[at, :] = spread(tau_ref[i : i + 1, :], scenarios)
    sigma[...] = spread(sigma_ref[...], scenarios)
    loads[1].wait()
    for k in range(slots):
        blocks_t[k] = blocks[k].T

    pl.semaphore_wait(barrier, len(peers))

    sent = []
    waited = [loads[2], loads[3]]
    stores = []

    def remote(src, dst, send_sem, recv_sem, peer):
        copy = pltpu.make_async_remote_copy(
            src_ref=src,
            dst_ref=dst,
            send_sem=send_sem,
            recv_sem=recv_sem,
            device_id=peer,
            device_id_type=MESH,
        )
        copy.start()
        sent.append(copy)
        return copy

    for it in range(ITERS):
        everyone, pair, outgoing = everyones[it], pairs[it], outgoings[it]
        plane_in, column_out, column_in = plane_ins[it], column_outs[it], column_ins[it]

        def pass_on(d, e):
            part = everyone.at[back_z(d), mine, :]
            return remote(
                part, part, gather_send.at[it, d, e], gather_recv.at[it, d, e], p_peer(e)
            )

        own_part = everyone.at[z, mine, :]
        along_z = [
            remote(
                own_part, own_part, gather_send.at[it, d, 0], gather_recv.at[it, d, 0], z_peer(d)
            )
            for d in range(1, zs)
        ]
        in_plane = [pass_on(0, e) for e in range(1, ps)]
        for d in range(1, zs):
            along_z[d - 1].wait_recv()
            in_plane += [pass_on(d, e) for e in range(1, ps)]
        for copy in in_plane:
            copy.wait_recv()

        for k in range(slots):
            terms[k] = jnp.dot(blocks_t[k], everyone[rows_of[k]], preferred_element_type=F32)
        exchanged = []
        for c in range(col_blocks):
            total = jnp.zeros((width, scenarios), F32)
            for k in range(slots):
                hit = jnp.logical_and(alive[k], cols_of[k] == c)
                total = total + jnp.where(hit, terms[k], 0.0)
            pair[row, c] = total.astype(BF16)
            part = pair.at[row, c]
            exchanged.append(
                [
                    remote(part, part, pair_send.at[it, f, c], pair_recv.at[it, f, c], r_peer(f))
                    for f in range(1, rs)
                ]
            )
        for load in waited:
            load.wait()
        waited = []
        for c in range(col_blocks):
            for copy in exchanged[c]:
                copy.wait_recv()
            at = pl.ds(c * width, width)
            back = pair[0, c].astype(F32)
            for r in range(1, rs):
                back = back + pair[r, c].astype(F32)
            old = primal[at, :]
            new = jnp.minimum(
                jnp.maximum(old - tau[at, :] * (cost[at, :] - back), 0.0), upper[at, :]
            )
            extrapolated[c] = (2.0 * new - old).astype(BF16)
            primal[at, :] = new
        if it == ITERS - 1:
            store = pltpu.make_async_copy(primal, primal_out, local_sem.at[0])
            store.start()
            stores.append(store)

        for k in range(slots):
            terms[k] = jnp.dot(blocks[k], extrapolated[cols_of[k]], preferred_element_type=F32)
        for g in range(zs):
            total = jnp.zeros((width, scenarios), F32)
            for k in range(slots):
                hit = jnp.logical_and(alive[k], rows_of[k] == g)
                total = total + jnp.where(hit, terms[k], 0.0)
            outgoing[g] = total.astype(BF16)
        planes = []
        for e in range(1, ps):
            theirs = pl.ds(pl.multiple_of(lax.rem(p + e, ps) * own, own), own)
            planes.append(
                remote(
                    outgoing.at[:, theirs, :],
                    plane_in.at[e - 1],
                    plane_send.at[it, e],
                    plane_recv.at[it, e],
                    p_peer(e),
                )
            )
        for copy in planes:
            copy.wait_recv()

        def plane_sum(g):
            total = outgoing[g, mine, :].astype(F32)
            for e in range(1, ps):
                total = total + plane_in[e - 1, g].astype(F32)
            return total

        columns = []
        for d in range(1, zs):
            column_out[d - 1] = plane_sum(lax.rem(z + d, zs)).astype(BF16)
            columns.append(
                remote(
                    column_out.at[d - 1],
                    column_in.at[d - 1],
                    column_send.at[it, d],
                    column_recv.at[it, d],
                    z_peer(d),
                )
            )
        forward = plane_sum(z)
        for d in range(1, zs):
            columns[d - 1].wait_recv()
            forward = forward + column_in[d - 1].astype(F32)
        new_dual = jnp.maximum(dual[...] + sigma[...] * (demand[...] - forward), 0.0)
        dual[...] = new_dual
        if it < ITERS - 1:
            everyones[it + 1][z, mine, :] = new_dual.astype(BF16)

    store = pltpu.make_async_copy(dual, dual_out.at[0], local_sem.at[1])
    store.start()
    stores.append(store)
    for copy in sent:
        copy.wait_send()
    for store in stores:
        store.wait()


def on_device(
    k_blocks,
    slot_row,
    slot_col,
    live_count,
    cost,
    upper,
    tau,
    sigma,
    demand,
    primal_start,
    dual_start,
):
    _, _, slots, width, _ = k_blocks.shape
    _, own, scenarios = dual_start.shape
    variables = primal_start.shape[0]
    col_blocks = variables // width
    rs = lax.axis_size("row")
    ps = width // own
    zs = lax.axis_size("col") // ps
    flat = lambda v: v.reshape(-1, 128)
    smem = pl.BlockSpec(memory_space=pltpu.SMEM)
    vmem = pl.BlockSpec(memory_space=pltpu.VMEM)
    anywhere = pl.BlockSpec(memory_space=pl.ANY)
    dma = pltpu.SemaphoreType.DMA
    twice = lambda shape, kind: [pltpu.VMEM(shape, kind) for _ in range(ITERS)]
    return pl.pallas_call(
        functools.partial(kernel, (zs, ps, rs)),
        out_shape=(
            jax.ShapeDtypeStruct(primal_start.shape, F32),
            jax.ShapeDtypeStruct(dual_start.shape, F32),
        ),
        in_specs=[smem] * 3 + [anywhere] + [vmem] * 4 + [anywhere] * 3,
        out_specs=(anywhere, anywhere),
        scratch_shapes=[
            pltpu.VMEM((slots, width, width), BF16),
            pltpu.VMEM((slots, width, width), BF16),
            pltpu.VMEM((variables, scenarios), F32),
            pltpu.VMEM((own, scenarios), F32),
            pltpu.VMEM((own, scenarios), F32),
            pltpu.VMEM((variables, scenarios), F32),
            pltpu.VMEM((variables, scenarios), F32),
            pltpu.VMEM((variables, scenarios), F32),
            pltpu.VMEM((own, scenarios), F32),
            pltpu.VMEM((slots, width, scenarios), F32),
            pltpu.VMEM((col_blocks, width, scenarios), BF16),
            twice((zs, width, scenarios), BF16),
            twice((rs, col_blocks, width, scenarios), BF16),
            twice((zs, width, scenarios), BF16),
            twice((ps - 1, zs, own, scenarios), BF16),
            twice((zs - 1, own, scenarios), BF16),
            twice((zs - 1, own, scenarios), BF16),
            dma((4,)),
            dma((ITERS, zs, ps)),
            dma((ITERS, zs, ps)),
            dma((ITERS, rs, col_blocks)),
            dma((ITERS, rs, col_blocks)),
            dma((ITERS, ps)),
            dma((ITERS, ps)),
            dma((ITERS, zs)),
            dma((ITERS, zs)),
        ],
        compiler_params=pltpu.CompilerParams(
            collective_id=0, has_side_effects=True, vmem_limit_bytes=40 * 1024 * 1024
        ),
        cost_estimate=pl.CostEstimate(
            flops=ITERS * 4 * slots * width * width * scenarios,
            bytes_accessed=2 * slots * width * width + 8 * variables * scenarios,
            transcendentals=0,
        ),
    )(
        slot_row,
        slot_col,
        live_count,
        k_blocks,
        flat(cost),
        flat(upper),
        flat(tau),
        sigma,
        demand,
        primal_start,
        dual_start,
    )


def solution(mesh):
    in_specs = (
        P("row", "col", None, None, None),
        P("row", "col", None),
        P("row", "col", None),
        P("row", "col"),
        P("col"),
        P("col"),
        P("col"),
        P("row", "col"),
        P("row", "col", None),
        P("col", None),
        P("row", "col", None),
    )
    out_specs = (P("col", None), P("row", "col", None))
    return jax.shard_map(
        on_device, mesh=mesh, in_specs=in_specs, out_specs=out_specs, check_vma=False
    )
```

```python
import functools

import jax
import jax.numpy as jnp
from jax import lax
from jax.experimental import pallas as pl
from jax.experimental.pallas import tpu as pltpu
from jax.sharding import PartitionSpec as P

ITERS = 2
MESH = pl.DeviceIdType.MESH
F32 = jnp.float32
BF16 = jnp.bfloat16


def spread(vector, lanes):
    n = vector.shape[1]
    at_row = lax.broadcasted_iota(jnp.int32, (n, n), 0)
    at_col = lax.broadcasted_iota(jnp.int32, (n, n), 1)
    picked = jnp.where(at_row == at_col, jnp.broadcast_to(vector, (n, n)), 0.0)
    return jnp.broadcast_to(jnp.sum(picked, axis=1, keepdims=True), (n, lanes))


def kernel(
    sizes,
    slot_row_hbm,
    slot_col_hbm,
    live_count_hbm,
    k_hbm,
    cost_hbm,
    upper_hbm,
    tau_hbm,
    sigma_hbm,
    demand_hbm,
    primal_hbm,
    dual_hbm,
    primal_out,
    dual_out,
    slot_row,
    slot_col,
    live_count,
    cost_ref,
    upper_ref,
    tau_ref,
    sigma_ref,
    blocks,
    blocks_t,
    primal,
    dual,
    demand,
    cost,
    upper,
    tau,
    sigma,
    terms,
    extrapolated,
    everyones,
    pairs,
    outgoings,
    totals,
    column_sums,
    ahead,
    plane_ins,
    column_outs,
    column_ins,
    last_outs,
    last_ins,
    local_sem,
    gather_send,
    gather_recv,
    pair_send,
    pair_recv,
    plane_send,
    plane_recv,
    column_send,
    column_recv,
    start_send,
    start_recv,
    last_send,
    last_recv,
):
    zs, ps, rs = sizes
    slots, width, _ = blocks.shape
    own = width // ps
    col_blocks = extrapolated.shape[0]
    scenarios = dual.shape[2]
    col = lax.axis_index("col")
    row = lax.axis_index("row")
    z, p = col // ps, lax.rem(col, ps)

    def z_peer(d):
        return {"col": lax.rem(z + d, zs) * ps + p}

    def p_peer(e):
        return {"col": z * ps + lax.rem(p + e, ps)}

    def r_peer(f):
        return {"row": lax.rem(row + f, rs)}

    def back_z(d):
        return lax.rem(z - d + zs, zs)

    mine = pl.ds(pl.multiple_of(p * own, own), own)

    loads = [
        pltpu.make_async_copy(src, dst, local_sem.at[i])
        for i, (src, dst) in enumerate(
            (
                (dual_hbm.at[0], dual.at[z]),
                (k_hbm.at[0, 0], blocks),
                (primal_hbm, primal),
                (demand_hbm.at[0], demand),
                (cost_hbm, cost_ref),
                (upper_hbm, upper_ref),
                (tau_hbm, tau_ref),
                (sigma_hbm, sigma_ref.at[z]),
                (slot_row_hbm, slot_row),
                (slot_col_hbm, slot_col),
                (live_count_hbm, live_count),
            )
        )
    ]
    for load in loads:
        load.start()

    barrier = pltpu.get_barrier_semaphore()
    peers = (
        [z_peer(d) for d in range(1, zs)]
        + [p_peer(e) for e in range(1, ps)]
        + [r_peer(f) for f in range(1, rs)]
    )
    for peer in peers:
        pl.semaphore_signal(barrier, inc=1, device_id=peer, device_id_type=MESH)

    loads[0].wait()
    everyones[0][z, mine, :] = dual[z].astype(BF16)

    for load in loads[3:8]:
        load.wait()
    chunk = cost_ref.shape[1]
    for i in range(cost_ref.shape[0]):
        at = pl.ds(i * chunk, chunk)
        cost[at, :] = spread(cost_ref[i : i + 1, :], scenarios)
        upper[at, :] = spread(upper_ref[i : i + 1, :], scenarios)
        tau[at, :] = spread(tau_ref[i : i + 1, :], scenarios)
    loads[1].wait()
    ahead[z] = dual[z] + spread(sigma_ref[z], scenarios) * demand[...]
    for k in range(slots):
        blocks_t[k] = blocks[k].T
    for load in loads[8:]:
        load.wait()
    live = live_count[0, 0]
    alive = [k < live for k in range(slots)]
    rows_of = [slot_row[0, 0, k] for k in range(slots)]
    cols_of = [slot_col[0, 0, k] for k in range(slots)]

    pl.semaphore_wait(barrier, len(peers))

    sent = []
    waited = [loads[2]]
    stores = []

    def remote(src, dst, send_sem, recv_sem, peer):
        copy = pltpu.make_async_remote_copy(
            src_ref=src,
            dst_ref=dst,
            send_sem=send_sem,
            recv_sem=recv_sem,
            device_id=peer,
            device_id_type=MESH,
        )
        copy.start()
        sent.append(copy)
        return copy

    for it in range(ITERS):
        everyone, pair, outgoing = everyones[it], pairs[it], outgoings[it]
        plane_in = plane_ins[it]

        def pass_on(g, e):
            part = everyone.at[g, mine, :]
            return remote(
                part, part, gather_send.at[it, g, e], gather_recv.at[it, g, e], p_peer(e)
            )

        in_plane = []
        if it == 0:
            own_part = everyone.at[z, mine, :]
            along_z = [
                remote(own_part, own_part, start_send.at[0, d], start_recv.at[0, d], z_peer(d))
                for d in range(1, zs)
            ]
            in_plane += [pass_on(z, e) for e in range(1, ps)]
            for d in range(1, zs):
                along_z[d - 1].wait_recv()
                in_plane += [pass_on(back_z(d), e) for e in range(1, ps)]
        else:
            for g in range(zs):
                forward = column_sums[g]
                for d in range(1, zs):
                    columns[g][d - 1].wait_recv()
                    forward = forward + column_ins[g, d - 1].astype(F32)
                new_dual = jnp.maximum(ahead[g] - sigma[g] * forward, 0.0)
                dual[g] = new_dual
                everyone[g, mine, :] = new_dual.astype(BF16)
                in_plane += [pass_on(g, e) for e in range(1, ps)]
        for copy in in_plane:
            copy.wait_recv()
        if it == 0:
            fetched = [
                remote(ref.at[z], ref.at[z], start_send.at[i, d], start_recv.at[i, d], z_peer(d))
                for i, ref in ((1, sigma_ref), (2, ahead))
                for d in range(1, zs)
            ]

        for k in range(slots):
            terms[k] = jnp.dot(blocks_t[k], everyone[rows_of[k]], preferred_element_type=F32)
        exchanged = []
        for c in range(col_blocks):
            total = jnp.zeros((width, scenarios), F32)
            for k in range(slots):
                hit = jnp.logical_and(alive[k], cols_of[k] == c)
                total = total + jnp.where(hit, terms[k], 0.0)
            pair[row, c] = total
            part = pair.at[row, c]
            exchanged.append(
                [
                    remote(part, part, pair_send.at[it, f, c], pair_recv.at[it, f, c], r_peer(f))
                    for f in range(1, rs)
                ]
            )
        for load in waited:
            load.wait()
        waited = []
        for c in range(col_blocks):
            for copy in exchanged[c]:
                copy.wait_recv()
            at = pl.ds(c * width, width)
            back = pair[0, c]
            for r in range(1, rs):
                back = back + pair[r, c]
            old = primal[at, :]
            new = jnp.minimum(
                jnp.maximum(old - tau[at, :] * (cost[at, :] - back), 0.0), upper[at, :]
            )
            extrapolated[c] = (2.0 * new - old).astype(BF16)
            primal[at, :] = new
        if it == ITERS - 1:
            store = pltpu.make_async_copy(primal, primal_out, local_sem.at[0])
            store.start()
            stores.append(store)

        for k in range(slots):
            terms[k] = jnp.dot(blocks[k], extrapolated[cols_of[k]], preferred_element_type=F32)
        planes = []
        order = list(range(zs))
        if it == ITERS - 1:
            order = [lax.rem(z + j, zs) for j in range(1, zs + 1)]
        for j, g in enumerate(order):
            total = jnp.zeros((width, scenarios), F32)
            for k in range(slots):
                hit = jnp.logical_and(alive[k], rows_of[k] == g)
                total = total + jnp.where(hit, terms[k], 0.0)
            totals[g] = total
            outgoing[g] = total.astype(BF16)
            planes.append([])
            for e in range(1, ps):
                theirs = pl.ds(pl.multiple_of(lax.rem(p + e, ps) * own, own), own)
                planes[j].append(
                    remote(
                        outgoing.at[g, theirs, :],
                        plane_in.at[e - 1, g],
                        plane_send.at[it, j, e],
                        plane_recv.at[it, j, e],
                        p_peer(e),
                    )
                )
        if it == 0:
            for copy in fetched:
                copy.wait_recv()
            for g in range(zs):
                sigma[g] = spread(sigma_ref[g], scenarios)

        columns = []
        for j, g in enumerate(order):
            total = totals[g, mine, :]
            for e in range(1, ps):
                planes[j][e - 1].wait_recv()
                total = total + plane_in[e - 1, g].astype(F32)
            if it < ITERS - 1:
                column_sums[g] = total
                column_outs[g] = total.astype(BF16)
                part = column_outs.at[g]
                columns.append(
                    [
                        remote(
                            part,
                            column_ins.at[g, d - 1],
                            column_send.at[g, d],
                            column_recv.at[g, d],
                            z_peer(d),
                        )
                        for d in range(1, zs)
                    ]
                )
            elif j < zs - 1:
                last_outs[j] = total.astype(BF16)
                columns.append(
                    remote(
                        last_outs.at[j],
                        last_ins.at[j],
                        last_send.at[j],
                        last_recv.at[j],
                        z_peer(j + 1),
                    )
                )
            else:
                forward = total
    for j, copy in enumerate(columns):
        copy.wait_recv()
        forward = forward + last_ins[j].astype(F32)
    dual[z] = jnp.maximum(dual[z] + sigma[z] * (demand[...] - forward), 0.0)

    store = pltpu.make_async_copy(dual.at[z], dual_out.at[0], local_sem.at[1])
    store.start()
    stores.append(store)
    for copy in sent:
        copy.wait_send()
    for store in stores:
        store.wait()


def on_device(
    k_blocks,
    slot_row,
    slot_col,
    live_count,
    cost,
    upper,
    tau,
    sigma,
    demand,
    primal_start,
    dual_start,
):
    _, _, slots, width, _ = k_blocks.shape
    _, own, scenarios = dual_start.shape
    variables = primal_start.shape[0]
    col_blocks = variables // width
    rs = lax.axis_size("row")
    ps = width // own
    zs = lax.axis_size("col") // ps
    flat = lambda v: v.reshape(-1, 128)
    anywhere = pl.BlockSpec(memory_space=pl.ANY)
    dma = pltpu.SemaphoreType.DMA
    twice = lambda shape, kind: [pltpu.VMEM(shape, kind) for _ in range(ITERS)]
    return pl.pallas_call(
        functools.partial(kernel, (zs, ps, rs)),
        out_shape=(
            jax.ShapeDtypeStruct(primal_start.shape, F32),
            jax.ShapeDtypeStruct(dual_start.shape, F32),
        ),
        in_specs=[anywhere] * 11,
        out_specs=(anywhere, anywhere),
        scratch_shapes=[
            pltpu.SMEM((1, 1, slots), jnp.int32),
            pltpu.SMEM((1, 1, slots), jnp.int32),
            pltpu.SMEM((1, 1), jnp.int32),
            pltpu.VMEM((variables // 128, 128), F32),
            pltpu.VMEM((variables // 128, 128), F32),
            pltpu.VMEM((variables // 128, 128), F32),
            pltpu.VMEM((zs, 1, own), F32),
            pltpu.VMEM((slots, width, width), BF16),
            pltpu.VMEM((slots, width, width), BF16),
            pltpu.VMEM((variables, scenarios), F32),
            pltpu.VMEM((zs, own, scenarios), F32),
            pltpu.VMEM((own, scenarios), F32),
            pltpu.VMEM((variables, scenarios), F32),
            pltpu.VMEM((variables, scenarios), F32),
            pltpu.VMEM((variables, scenarios), F32),
            pltpu.VMEM((zs, own, scenarios), F32),
            pltpu.VMEM((slots, width, scenarios), F32),
            pltpu.VMEM((col_blocks, width, scenarios), BF16),
            twice((zs, width, scenarios), BF16),
            twice((rs, col_blocks, width, scenarios), F32),
            twice((zs, width, scenarios), BF16),
            pltpu.VMEM((zs, width, scenarios), F32),
            pltpu.VMEM((zs, own, scenarios), F32),
            pltpu.VMEM((zs, own, scenarios), F32),
            twice((ps - 1, zs, own, scenarios), BF16),
            pltpu.VMEM((zs, own, scenarios), BF16),
            pltpu.VMEM((zs, zs - 1, own, scenarios), BF16),
            pltpu.VMEM((zs - 1, own, scenarios), BF16),
            pltpu.VMEM((zs - 1, own, scenarios), BF16),
            dma((11,)),
            dma((ITERS, zs, ps)),
            dma((ITERS, zs, ps)),
            dma((ITERS, rs, col_blocks)),
            dma((ITERS, rs, col_blocks)),
            dma((ITERS, zs, ps)),
            dma((ITERS, zs, ps)),
            dma((zs, zs)),
            dma((zs, zs)),
            dma((4, zs)),
            dma((4, zs)),
            dma((zs,)),
            dma((zs,)),
        ],
        compiler_params=pltpu.CompilerParams(
            collective_id=0, has_side_effects=True, vmem_limit_bytes=60 * 1024 * 1024
        ),
        cost_estimate=pl.CostEstimate(
            flops=ITERS * 4 * slots * width * width * scenarios,
            bytes_accessed=2 * slots * width * width + 8 * variables * scenarios,
            transcendentals=0,
        ),
    )(
        slot_row,
        slot_col,
        live_count,
        k_blocks,
        flat(cost),
        flat(upper),
        flat(tau),
        sigma,
        demand,
        primal_start,
        dual_start,
    )


def solution(mesh):
    in_specs = (
        P("row", "col", None, None, None),
        P("row", "col", None),
        P("row", "col", None),
        P("row", "col"),
        P("col"),
        P("col"),
        P("col"),
        P("row", "col"),
        P("row", "col", None),
        P("col", None),
        P("row", "col", None),
    )
    out_specs = (P("col", None), P("row", "col", None))
    return jax.shard_map(
        on_device, mesh=mesh, in_specs=in_specs, out_specs=out_specs, check_vma=False
    )
```

```python
import functools

import jax
import jax.numpy as jnp
from jax import lax
from jax.experimental import pallas as pl
from jax.experimental.pallas import tpu as pltpu
from jax.sharding import PartitionSpec as P

ITERS = 2
MESH = pl.DeviceIdType.MESH
F32 = jnp.float32
BF16 = jnp.bfloat16


def spread(vector, lanes):
    n = vector.shape[1]
    at_row = lax.broadcasted_iota(jnp.int32, (n, n), 0)
    at_col = lax.broadcasted_iota(jnp.int32, (n, n), 1)
    picked = jnp.where(at_row == at_col, jnp.broadcast_to(vector, (n, n)), 0.0)
    return jnp.broadcast_to(jnp.sum(picked, axis=1, keepdims=True), (n, lanes))


def kernel(
    sizes,
    slot_row_hbm,
    slot_col_hbm,
    live_count_hbm,
    k_hbm,
    cost_hbm,
    upper_hbm,
    tau_hbm,
    sigma_hbm,
    demand_hbm,
    primal_hbm,
    dual_hbm,
    primal_out,
    dual_out,
    slot_row,
    slot_col,
    live_count,
    cost_ref,
    upper_ref,
    tau_ref,
    sigma_ref,
    blocks,
    blocks_t,
    primal,
    dual,
    demand,
    cost,
    upper,
    tau,
    sigma,
    terms,
    extrapolated,
    everyones,
    pairs,
    outgoings,
    totals,
    column_sums,
    ahead,
    plane_ins,
    column_outs,
    column_ins,
    last_outs,
    last_ins,
    local_sem,
    gather_send,
    gather_recv,
    pair_send,
    pair_recv,
    plane_send,
    plane_recv,
    column_send,
    column_recv,
    start_send,
    start_recv,
    last_send,
    last_recv,
):
    zs, ps, rs = sizes
    slots, width, _ = blocks.shape
    own = width // ps
    col_blocks = extrapolated.shape[0]
    scenarios = dual.shape[2]
    col = lax.axis_index("col")
    row = lax.axis_index("row")
    z, p = col // ps, lax.rem(col, ps)

    def z_peer(d):
        return {"col": lax.rem(z + d, zs) * ps + p}

    def p_peer(e):
        return {"col": z * ps + lax.rem(p + e, ps)}

    def r_peer(f):
        return {"row": lax.rem(row + f, rs)}

    def back_z(d):
        return lax.rem(z - d + zs, zs)

    mine = pl.ds(pl.multiple_of(p * own, own), own)

    loads = [
        pltpu.make_async_copy(src, dst, local_sem.at[i])
        for i, (src, dst) in enumerate(
            (
                (dual_hbm.at[0], dual.at[z]),
                (k_hbm.at[0, 0], blocks),
                (primal_hbm, primal),
                (demand_hbm.at[0], demand),
                (cost_hbm, cost_ref),
                (upper_hbm, upper_ref),
                (tau_hbm, tau_ref),
                (sigma_hbm, sigma_ref.at[z]),
                (slot_row_hbm, slot_row),
                (slot_col_hbm, slot_col),
                (live_count_hbm, live_count),
            )
        )
    ]
    for load in loads:
        load.start()

    barrier = pltpu.get_barrier_semaphore()
    peers = (
        [z_peer(d) for d in range(1, zs)]
        + [p_peer(e) for e in range(1, ps)]
        + [r_peer(f) for f in range(1, rs)]
    )
    for peer in peers:
        pl.semaphore_signal(barrier, inc=1, device_id=peer, device_id_type=MESH)

    loads[0].wait()
    everyones[0][z, mine, :] = dual[z].astype(BF16)

    pl.semaphore_wait(barrier, len(peers))

    sent = []
    waited = [loads[2]]
    stores = []

    def remote(src, dst, send_sem, recv_sem, peer):
        copy = pltpu.make_async_remote_copy(
            src_ref=src,
            dst_ref=dst,
            send_sem=send_sem,
            recv_sem=recv_sem,
            device_id=peer,
            device_id_type=MESH,
        )
        copy.start()
        sent.append(copy)
        return copy

    for it in range(ITERS):
        everyone, pair, outgoing = everyones[it], pairs[it], outgoings[it]
        plane_in = plane_ins[it]

        def pass_on(g, e):
            part = everyone.at[g, mine, :]
            return remote(
                part, part, gather_send.at[it, g, e], gather_recv.at[it, g, e], p_peer(e)
            )

        in_plane = []
        if it == 0:
            own_part = everyone.at[z, mine, :]
            along_z = [
                remote(own_part, own_part, start_send.at[0, d], start_recv.at[0, d], z_peer(d))
                for d in range(1, zs)
            ]
            in_plane += [pass_on(z, e) for e in range(1, ps)]
            loads[1].wait()
            for k in range(slots):
                blocks_t[k] = blocks[k].T
            for d in range(1, zs):
                along_z[d - 1].wait_recv()
                in_plane += [pass_on(back_z(d), e) for e in range(1, ps)]
            for load in loads[8:]:
                load.wait()
            live = live_count[0, 0]
            alive = [k < live for k in range(slots)]
            rows_of = [slot_row[0, 0, k] for k in range(slots)]
            cols_of = [slot_col[0, 0, k] for k in range(slots)]

            for load in loads[3:8]:
                load.wait()
            chunk = cost_ref.shape[1]
            for i in range(cost_ref.shape[0]):
                at = pl.ds(i * chunk, chunk)
                cost[at, :] = spread(cost_ref[i : i + 1, :], scenarios)
                upper[at, :] = spread(upper_ref[i : i + 1, :], scenarios)
                tau[at, :] = spread(tau_ref[i : i + 1, :], scenarios)
            ahead[z] = dual[z] + spread(sigma_ref[z], scenarios) * demand[...]
        else:
            for g in range(zs):
                forward = column_sums[g]
                for d in range(1, zs):
                    columns[g][d - 1].wait_recv()
                    forward = forward + column_ins[g, d - 1].astype(F32)
                new_dual = jnp.maximum(ahead[g] - sigma[g] * forward, 0.0)
                dual[g] = new_dual
                everyone[g, mine, :] = new_dual.astype(BF16)
                in_plane += [pass_on(g, e) for e in range(1, ps)]
        for copy in in_plane:
            copy.wait_recv()
        if it == 0:
            fetched = [
                remote(ref.at[z], ref.at[z], start_send.at[i, d], start_recv.at[i, d], z_peer(d))
                for i, ref in ((1, sigma_ref), (2, ahead))
                for d in range(1, zs)
            ]

        for k in range(slots):
            terms[k] = jnp.dot(blocks_t[k], everyone[rows_of[k]], preferred_element_type=F32)
        exchanged = []
        for c in range(col_blocks):
            total = jnp.zeros((width, scenarios), F32)
            for k in range(slots):
                hit = jnp.logical_and(alive[k], cols_of[k] == c)
                total = total + jnp.where(hit, terms[k], 0.0)
            pair[row, c] = total
            part = pair.at[row, c]
            exchanged.append(
                [
                    remote(part, part, pair_send.at[it, f, c], pair_recv.at[it, f, c], r_peer(f))
                    for f in range(1, rs)
                ]
            )
        for load in waited:
            load.wait()
        waited = []
        for c in range(col_blocks):
            for copy in exchanged[c]:
                copy.wait_recv()
            at = pl.ds(c * width, width)
            back = pair[0, c]
            for r in range(1, rs):
                back = back + pair[r, c]
            old = primal[at, :]
            new = jnp.minimum(
                jnp.maximum(old - tau[at, :] * (cost[at, :] - back), 0.0), upper[at, :]
            )
            extrapolated[c] = (2.0 * new - old).astype(BF16)
            primal[at, :] = new
        if it == ITERS - 1:
            store = pltpu.make_async_copy(primal, primal_out, local_sem.at[0])
            store.start()
            stores.append(store)

        for k in range(slots):
            terms[k] = jnp.dot(blocks[k], extrapolated[cols_of[k]], preferred_element_type=F32)
        planes = []
        order = list(range(zs))
        if it == ITERS - 1:
            order = [lax.rem(z + j, zs) for j in range(1, zs + 1)]
        for j, g in enumerate(order):
            total = jnp.zeros((width, scenarios), F32)
            for k in range(slots):
                hit = jnp.logical_and(alive[k], rows_of[k] == g)
                total = total + jnp.where(hit, terms[k], 0.0)
            totals[g] = total
            outgoing[g] = total.astype(BF16)
            planes.append([])
            for e in range(1, ps):
                theirs = pl.ds(pl.multiple_of(lax.rem(p + e, ps) * own, own), own)
                planes[j].append(
                    remote(
                        outgoing.at[g, theirs, :],
                        plane_in.at[e - 1, g],
                        plane_send.at[it, j, e],
                        plane_recv.at[it, j, e],
                        p_peer(e),
                    )
                )
        if it == 0:
            for copy in fetched:
                copy.wait_recv()
            for g in range(zs):
                sigma[g] = spread(sigma_ref[g], scenarios)

        columns = []
        for j, g in enumerate(order):
            total = totals[g, mine, :]
            for e in range(1, ps):
                planes[j][e - 1].wait_recv()
                total = total + plane_in[e - 1, g].astype(F32)
            if it < ITERS - 1:
                column_sums[g] = total
                column_outs[g] = total.astype(BF16)
                part = column_outs.at[g]
                columns.append(
                    [
                        remote(
                            part,
                            column_ins.at[g, d - 1],
                            column_send.at[g, d],
                            column_recv.at[g, d],
                            z_peer(d),
                        )
                        for d in range(1, zs)
                    ]
                )
            elif j < zs - 1:
                last_outs[j] = total.astype(BF16)
                columns.append(
                    remote(
                        last_outs.at[j],
                        last_ins.at[j],
                        last_send.at[j],
                        last_recv.at[j],
                        z_peer(j + 1),
                    )
                )
            else:
                forward = total
    for j, copy in enumerate(columns):
        copy.wait_recv()
        forward = forward + last_ins[j].astype(F32)
    dual[z] = jnp.maximum(dual[z] + sigma[z] * (demand[...] - forward), 0.0)

    store = pltpu.make_async_copy(dual.at[z], dual_out.at[0], local_sem.at[1])
    store.start()
    stores.append(store)
    for copy in sent:
        copy.wait_send()
    for store in stores:
        store.wait()


def on_device(
    k_blocks,
    slot_row,
    slot_col,
    live_count,
    cost,
    upper,
    tau,
    sigma,
    demand,
    primal_start,
    dual_start,
):
    _, _, slots, width, _ = k_blocks.shape
    _, own, scenarios = dual_start.shape
    variables = primal_start.shape[0]
    col_blocks = variables // width
    rs = lax.axis_size("row")
    ps = width // own
    zs = lax.axis_size("col") // ps
    flat = lambda v: v.reshape(-1, 128)
    anywhere = pl.BlockSpec(memory_space=pl.ANY)
    dma = pltpu.SemaphoreType.DMA
    twice = lambda shape, kind: [pltpu.VMEM(shape, kind) for _ in range(ITERS)]
    return pl.pallas_call(
        functools.partial(kernel, (zs, ps, rs)),
        out_shape=(
            jax.ShapeDtypeStruct(primal_start.shape, F32),
            jax.ShapeDtypeStruct(dual_start.shape, F32),
        ),
        in_specs=[anywhere] * 11,
        out_specs=(anywhere, anywhere),
        scratch_shapes=[
            pltpu.SMEM((1, 1, slots), jnp.int32),
            pltpu.SMEM((1, 1, slots), jnp.int32),
            pltpu.SMEM((1, 1), jnp.int32),
            pltpu.VMEM((variables // 128, 128), F32),
            pltpu.VMEM((variables // 128, 128), F32),
            pltpu.VMEM((variables // 128, 128), F32),
            pltpu.VMEM((zs, 1, own), F32),
            pltpu.VMEM((slots, width, width), BF16),
            pltpu.VMEM((slots, width, width), BF16),
            pltpu.VMEM((variables, scenarios), F32),
            pltpu.VMEM((zs, own, scenarios), F32),
            pltpu.VMEM((own, scenarios), F32),
            pltpu.VMEM((variables, scenarios), F32),
            pltpu.VMEM((variables, scenarios), F32),
            pltpu.VMEM((variables, scenarios), F32),
            pltpu.VMEM((zs, own, scenarios), F32),
            pltpu.VMEM((slots, width, scenarios), F32),
            pltpu.VMEM((col_blocks, width, scenarios), BF16),
            twice((zs, width, scenarios), BF16),
            twice((rs, col_blocks, width, scenarios), F32),
            twice((zs, width, scenarios), BF16),
            pltpu.VMEM((zs, width, scenarios), F32),
            pltpu.VMEM((zs, own, scenarios), F32),
            pltpu.VMEM((zs, own, scenarios), F32),
            twice((ps - 1, zs, own, scenarios), BF16),
            pltpu.VMEM((zs, own, scenarios), BF16),
            pltpu.VMEM((zs, zs - 1, own, scenarios), BF16),
            pltpu.VMEM((zs - 1, own, scenarios), BF16),
            pltpu.VMEM((zs - 1, own, scenarios), BF16),
            dma((11,)),
            dma((ITERS, zs, ps)),
            dma((ITERS, zs, ps)),
            dma((ITERS, rs, col_blocks)),
            dma((ITERS, rs, col_blocks)),
            dma((ITERS, zs, ps)),
            dma((ITERS, zs, ps)),
            dma((zs, zs)),
            dma((zs, zs)),
            dma((4, zs)),
            dma((4, zs)),
            dma((zs,)),
            dma((zs,)),
        ],
        compiler_params=pltpu.CompilerParams(
            collective_id=0, has_side_effects=True, vmem_limit_bytes=60 * 1024 * 1024
        ),
        cost_estimate=pl.CostEstimate(
            flops=ITERS * 4 * slots * width * width * scenarios,
            bytes_accessed=2 * slots * width * width + 8 * variables * scenarios,
            transcendentals=0,
        ),
    )(
        slot_row,
        slot_col,
        live_count,
        k_blocks,
        flat(cost),
        flat(upper),
        flat(tau),
        sigma,
        demand,
        primal_start,
        dual_start,
    )


def solution(mesh):
    in_specs = (
        P("row", "col", None, None, None),
        P("row", "col", None),
        P("row", "col", None),
        P("row", "col"),
        P("col"),
        P("col"),
        P("col"),
        P("row", "col"),
        P("row", "col", None),
        P("col", None),
        P("row", "col", None),
    )
    out_specs = (P("col", None), P("row", "col", None))
    return jax.shard_map(
        on_device, mesh=mesh, in_specs=in_specs, out_specs=out_specs, check_vma=False
    )
```
